32 devices in a mesh: space: 8 (over z, y), chan: 4 (over x, core).
Axes of the slice: x: 2, y: 2, z: 4, core: 2. Of those that a mesh axis runs over, the one named last changes fastest.
Arguments:
- inputs: bfloat16 [128, 16, 16, 128], P('chan', 'space'), may hold values from -6 to 6
- weight: bfloat16 [128, 27, 128], P(None, None, 'chan'), may hold values from -0.109375 to 0.109375
- cotangent: bfloat16 [128, 16, 16, 128], P('chan', 'space'), may hold values from -6 to 6
Outputs:
- output: bfloat16 [128, 16, 16, 128], P('chan', 'space')
- grad_inputs: bfloat16 [128, 16, 16, 128], P('chan', 'space')
- grad_weight: float32 [128, 27, 128], P('space', None, 'chan')
The draws below stay inside these ranges and needn't reach their ends.
All inputs are finite; a program needn't handle non-finite values.
Results may differ from the reference program's by a relative error of at most 0.0085.
Values may be sent and summed in bfloat16 or wider, within the bound.
A program may use at most 64 MiB of HBM per device.

```python
import jax
import jax.numpy as jnp

CH = 128
TAPS = 27
H = 16
W = 128
DEPTH = 16


def shard_levels(rng, dims, shards, least, top_value):
    def one(position, parts):
        steps = jax.random.uniform(jax.random.fold_in(jax.random.fold_in(rng, 6), position), (parts,), jnp.float32, least / len(shards), top_value / len(shards))
        return jnp.repeat(jnp.exp(steps), dims[position] // parts).reshape((-1,) + (1,) * (len(dims) - position - 1))

    loudness = one(*shards[0])
    for cut in shards[1:]:
        loudness = loudness * one(*cut)
    return loudness


def normal_values(rng, dims, spread, reach, cuts=(), kind=jnp.bfloat16):
    values = jax.random.normal(rng, dims, jnp.float32) * spread
    if len(cuts) > 0:
        values = shard_levels(rng, dims, cuts, -0.22, 0.18) * values
    return jnp.clip(values, min=-reach, max=reach).astype(kind)


def setup_inputs(seed: int = 0) -> dict:
    streams_of = jax.random.split(jax.random.key(seed), 4)
    return {
        "inputs": normal_values(streams_of[0], (CH, DEPTH, H, W), 1.0, 6.0, ((0, 4), (1, 8))),
        "weight": normal_values(streams_of[1], (CH, TAPS, CH), (CH * TAPS) ** -0.5, 0.109375, ((2, 4),)),
        "cotangent": normal_values(streams_of[2], (CH, DEPTH, H, W), 1.0, 6.0, ((0, 4), (1, 8))),
    }


def tap_offsets():
    return [(shift_d, shift_h, shift_w) for shift_d in (-1, 0, 1) for shift_h in (-1, 0, 1) for shift_w in (-1, 0, 1)]


def reference(inputs, weight, cotangent):
    values = inputs.astype(jnp.float32)
    filters = weight.astype(jnp.float32)
    pre_act = jnp.zeros(inputs.shape, jnp.float32)
    for index_tap, (shift_d, shift_h, shift_w) in enumerate(tap_offsets()):
        moved = jnp.roll(values, (-shift_d, -shift_h, -shift_w), axis=(1, 2, 3))
        pre_act = pre_act + jnp.einsum('idhw,io->odhw', moved, filters[:, index_tap, :])
    output = jnp.maximum(pre_act, 0.0).astype(jnp.bfloat16)
    grad_pre = jnp.where(pre_act > 0, cotangent.astype(jnp.float32), 0.0).astype(jnp.bfloat16)
    grad_values = grad_pre.astype(jnp.float32)
    grad_inputs = jnp.zeros(inputs.shape, jnp.float32)
    tap_grads = []
    for index_tap, (shift_d, shift_h, shift_w) in enumerate(tap_offsets()):
        term = jnp.einsum('odhw,io->idhw', grad_values, filters[:, index_tap, :])
        grad_inputs = grad_inputs + jnp.roll(term, (shift_d, shift_h, shift_w), axis=(1, 2, 3))
        moved = jnp.roll(values, (-shift_d, -shift_h, -shift_w), axis=(1, 2, 3))
        tap_grads.append(jnp.einsum('idhw,odhw->io', moved, grad_values))
    grad_weight = jnp.stack(tap_grads, axis=1)
    return output, grad_inputs.astype(jnp.bfloat16), grad_weight
```

```python
import functools

import jax
import jax.numpy as jnp
from jax import lax
from jax.experimental import pallas as pl
from jax.experimental.pallas import tpu as pltpu
from jax.sharding import PartitionSpec as P


def padded(cells, sides, width):
    for axis, dim in sides:
        count = lax.axis_size(axis)
        head = lax.slice_in_dim(cells, 0, width, axis=dim)
        tail = lax.slice_in_dim(cells, cells.shape[dim] - width, cells.shape[dim], axis=dim)
        cells = jnp.concatenate(
            [
                lax.ppermute(tail, axis, [(i, (i + 1) % count) for i in range(count)]),
                cells,
                lax.ppermute(head, axis, [((i + 1) % count, i) for i in range(count)]),
            ],
            axis=dim,
        )
    return cells


def tap_offsets():
    return [
        (shift_d, shift_h, shift_w)
        for shift_d in (-1, 0, 1)
        for shift_h in (-1, 0, 1)
        for shift_w in (-1, 0, 1)
    ]


def per_device(inputs, weight, cotangent):
    depth_local = inputs.shape[1]
    moved_inputs, moved_cot = (
        lax.all_to_all(inputs, "chan", split_axis=2, concat_axis=0, tiled=True),
        lax.all_to_all(cotangent, "chan", split_axis=2, concat_axis=0, tiled=True),
    )
    rows_local = moved_inputs.shape[2]
    extended = padded(moved_inputs, (("space", 1), ("chan", 2)), 1)
    filters = lax.all_gather(weight, "chan", axis=2, tiled=True)
    pre_act = jnp.zeros(moved_inputs.shape, jnp.float32)
    for index_tap, (shift_d, shift_h, shift_w) in enumerate(tap_offsets()):
        piece = extended[
            :, 1 + shift_d : 1 + shift_d + depth_local, 1 + shift_h : 1 + shift_h + rows_local
        ]
        piece = jnp.roll(piece, -shift_w, axis=3)
        pre_act = pre_act + jnp.einsum(
            "idhw,io->odhw", piece, filters[:, index_tap, :], preferred_element_type=jnp.float32
        )
    out_local = jnp.maximum(pre_act, 0.0).astype(jnp.bfloat16)
    grad_pre = jnp.where(pre_act > 0, moved_cot.astype(jnp.float32), 0.0).astype(jnp.bfloat16)
    output = lax.all_to_all(out_local, "chan", split_axis=0, concat_axis=2, tiled=True)
    grad_ext = padded(grad_pre, (("space", 1), ("chan", 2)), 1)
    grad_sum = jnp.zeros(moved_inputs.shape, jnp.float32)
    for index_tap, (shift_d, shift_h, shift_w) in enumerate(tap_offsets()):
        piece = grad_ext[
            :, 1 - shift_d : 1 - shift_d + depth_local, 1 - shift_h : 1 - shift_h + rows_local
        ]
        piece = jnp.roll(piece, shift_w, axis=3)
        grad_sum = grad_sum + jnp.einsum(
            "odhw,io->idhw", piece, filters[:, index_tap, :], preferred_element_type=jnp.float32
        )
    grad_inputs = lax.all_to_all(
        grad_sum.astype(jnp.bfloat16), "chan", split_axis=0, concat_axis=2, tiled=True
    )
    tap_list = []
    for index_tap, (shift_d, shift_h, shift_w) in enumerate(tap_offsets()):
        piece = extended[
            :, 1 + shift_d : 1 + shift_d + depth_local, 1 + shift_h : 1 + shift_h + rows_local
        ]
        piece = jnp.roll(piece, -shift_w, axis=3)
        tap_list.append(
            jnp.einsum("idhw,odhw->io", piece, grad_pre, preferred_element_type=jnp.float32)
        )
    partial_sum = lax.psum_scatter(
        jnp.stack(tap_list, axis=1), "space", scatter_dimension=0, tiled=True
    )
    grad_weight = lax.psum_scatter(partial_sum, "chan", scatter_dimension=2, tiled=True)
    return (output, grad_inputs, grad_weight)


MESH = pl.DeviceIdType.MESH


def stencil(filters, cells, total):
    rows = cells.shape[0]
    depth = cells.shape[1] * cells.shape[2] * cells.shape[3]
    total[...] = jnp.zeros_like(total)

    @pl.loop(0, rows // 2)
    def _(pair):
        right = jnp.concatenate(
            [cells[2 * pair].reshape(depth, 128), cells[2 * pair + 1].reshape(depth, 128)], axis=1
        )
        terms = jnp.dot(filters(), right, preferred_element_type=jnp.float32)
        for half in range(2):
            part = terms[:, 128 * half : 128 * half + 128].reshape(2, 9, 32, 128)
            for b in range(3):
                one = [part[:, 3 * b + c].reshape(64, 128) for c in range(3)]
                row = lax.rem(2 * pair + half + rows + 1 - b, rows)
                total[row] += one[1] + pltpu.roll(one[0], 1, 1) + pltpu.roll(one[2], 127, 1)


def kernel(
    spaces, x_ref, cot_ref, wf_ref, wg_ref, out_ref, gi_ref, gw_ref,
    xg, gp, wf, wg, cot, rolled, total, parts, other, sums, landed, part_out,
    send, recv, local,
):
    s, c = lax.axis_index("space"), lax.axis_index("chan")
    x, k = c // 2, lax.rem(c, 2)
    chan = [c, 2 * x + 1 - k, lax.rem(c + 2, 4), 2 * (1 - x) + 1 - k]
    up, down = lax.rem(s + 1, spaces), lax.rem(s + spaces - 1, spaces)

    barrier = pltpu.get_barrier_semaphore()
    greeted = [(s, other_c) for other_c in chan[1:]]
    greeted += [(side, other_c) for side in (up, down) for other_c in range(4)]
    greeted += [(lax.rem(s + step, spaces), c) for step in range(2, spaces - 1)]
    for device in greeted:
        pl.semaphore_signal(barrier, inc=1, device_id=device, device_id_type=MESH)
    pl.semaphore_wait(barrier, len(greeted))

    def start(src, dst, out_sem, in_sem, device):
        copy = pltpu.make_async_remote_copy(
            src_ref=src, dst_ref=dst, send_sem=send.at[out_sem], recv_sem=recv.at[in_sem],
            device_id=device, device_id_type=MESH,
        )
        copy.start()
        return copy

    def wait_in(dst, in_sem):
        pltpu.make_async_copy(dst, dst, recv.at[in_sem]).wait()

    sent = []
    keep = [
        pltpu.make_async_copy(x_ref, xg.at[:, c, pl.ds(1 - k, 2)], local.at[0]),
        pltpu.make_async_copy(cot_ref.at[:, k], cot.at[:, k], local.at[1]),
        pltpu.make_async_copy(wf_ref, wf.at[k], local.at[2]),
        pltpu.make_async_copy(wg_ref.at[x], wg.at[c], local.at[3]),
    ]
    for copy in keep:
        copy.start()
    for j in (2, 3, 1):
        core = k if j == 2 else 1 - k
        sent.append(start(x_ref, xg.at[:, c, pl.ds(1 - core, 2)], j - 1, j - 1, (s, chan[j])))
    for plane, side in ((0, down), (1, up)):
        for to_x in range(2):
            sent.append(
                start(
                    x_ref.at[:, plane], xg.at[:, c, 2 * (1 - plane)],
                    3 + 2 * plane + to_x, 3 + c, (side, 2 * to_x + 1 - plane),
                )
            )
    sent.append(start(wf_ref, wf.at[k], 7, 7, (s, chan[1])))
    sent.append(start(cot_ref.at[:, 1 - k], cot.at[:, k], 8, 8, (s, chan[1])))
    for j in (2, 3, 1):
        sent.append(start(wg_ref.at[chan[j] // 2], wg.at[c], 8 + j, 8 + j, (s, chan[j])))

    zero = jnp.zeros((4, 32, 128), jnp.bfloat16)

    @pl.loop(0, xg.shape[0])
    def _(h):
        xg[h, :, 3] = zero
        gp[h, :, 3] = zero
        rolled[h, :, 3] = zero[:2]

    for copy in keep:
        copy.wait()
    for j in (1, 2, 3):
        wait_in(xg.at[:, chan[j], pl.ds(1 - k, 2)], j - 1)
    for from_c in range(4):
        wait_in(xg.at[:, from_c, 2 * k], 3 + from_c)
    wait_in(wf.at[1 - k], 7)
    stencil(lambda: wf[...].reshape(576, 512), xg, total)
    wait_in(cot.at[:, 1 - k], 8)

    @pl.loop(0, xg.shape[0])
    def _(h):
        pre = total[h].reshape(2, 32, 128)
        out = jnp.maximum(pre, 0.0).astype(jnp.bfloat16)
        part_out[h] = out
        grad = jnp.where(pre > 0, cot[h].astype(jnp.float32), 0.0)
        gp[h, pl.ds(2 * x, 2), 1] = grad.astype(jnp.bfloat16)
        flat = grad.reshape(64, 128)
        rolled[h, :, 0] = pltpu.roll(flat, 127, 1).reshape(2, 32, 128).astype(jnp.bfloat16)
        rolled[h, :, 1] = grad.astype(jnp.bfloat16)
        rolled[h, :, 2] = pltpu.roll(flat, 1, 1).reshape(2, 32, 128).astype(jnp.bfloat16)

    mine = gp.at[:, pl.ds(2 * x, 2), 1]

    def place(slot):
        return gp.at[:, pl.ds(2 * x, 2), slot]

    side = lax.rem(s + spaces + 2 * k - 1, spaces)
    sent.append(start(mine, place(1), 13, 13, (s, chan[2])))
    sent.append(start(mine, place(2 * k), 14, 14, (s, chan[3])))
    for to_x in range(2):
        sent.append(start(mine, place(2 * (1 - k)), 15 + to_x, 15 + x, (side, 2 * to_x + 1 - k)))
    sent.append(start(mine, place(2 * k), 12, 12, (s, chan[1])))
    sent.append(start(part_out.at[:, 1 - k], out_ref.at[:, k], 17, 17, (s, chan[1])))
    copy_out = pltpu.make_async_copy(part_out.at[:, k], out_ref.at[:, k], local.at[0])
    copy_out.start()

    rows = xg.shape[0]

    @pl.loop(0, 3)
    def _(b):
        left = jnp.concatenate(
            [xg[lax.rem(h + rows + b - 1, rows)].reshape(512, 128) for h in range(rows)], axis=1
        )
        right = jnp.concatenate([rolled[h].reshape(256, 128) for h in range(rows)], axis=1)
        got = lax.dot_general(
            left, right, (((1,), (1,)), ((), ())), preferred_element_type=jnp.float32
        ).astype(jnp.bfloat16)
        for half in range(2):
            parts[half, b] = got[:, 128 * half : 128 * half + 128].reshape(4, 4, 32, 128)[:, :3]

    sent.append(start(parts.at[1 - k], other, 18, 18, (s, chan[1])))
    wait_in(other, 18)

    @pl.loop(0, 3)
    def _(b):
        sums[b] = (
            parts[k, b].astype(jnp.float32) + other[b].astype(jnp.float32)
        ).astype(jnp.bfloat16)

    def block(owner):
        return sums.at[:, owner // 2, :, pl.ds(pl.multiple_of(16 * lax.rem(owner, 2), 16), 16)]

    for step in range(1, spaces):
        owner = lax.rem(s + step, spaces)
        sent.append(start(block(owner), landed.at[step], 18 + step, 18 + step, (owner, c)))
    own = pltpu.make_async_copy(block(s), landed.at[0], local.at[1])
    own.start()

    wait_in(place(1), 12)
    wait_in(place(1), 13)
    wait_in(place(1), 14)
    for from_x in range(2):
        wait_in(place(1), 15 + from_x)
    for j in (1, 2, 3):
        wait_in(wg.at[0], 8 + j)
    stencil(lambda: jnp.concatenate([wg[j] for j in range(4)], axis=1), gp, total)

    @pl.loop(0, rows)
    def _(h):
        part_gi = total[h].reshape(2, 32, 128).astype(jnp.bfloat16)
        rolled[h, :, 0] = part_gi

    sent.append(start(rolled.at[:, 1 - k, 0], gi_ref.at[:, k], 18 + spaces, 18 + spaces, (s, chan[1])))
    copy_gi = pltpu.make_async_copy(rolled.at[:, k, 0], gi_ref.at[:, k], local.at[2])
    copy_gi.start()

    own.wait()
    for step in range(1, spaces):
        wait_in(landed.at[step], 18 + step)
    whole = landed[0].astype(jnp.float32)
    for step in range(1, spaces):
        whole = whole + landed[step].astype(jnp.float32)
    gw_ref[...] = whole

    copy_out.wait()
    copy_gi.wait()
    wait_in(out_ref.at[:, 1 - k], 17)
    wait_in(gi_ref.at[:, 1 - k], 18 + spaces)
    for copy in sent:
        copy.wait_send()


def fused(inputs, weight, cotangent):
    spaces = lax.axis_size("space")
    count, planes, rows, cols = inputs.shape
    taps = weight.reshape(4, 32, 3, 3, 3, 32)
    wf = jnp.pad(
        jnp.transpose(taps, (3, 4, 5, 0, 2, 1)), ((0, 0),) * 4 + ((0, 1), (0, 0))
    ).reshape(288, 512)
    flipped = taps[:, :, ::-1, ::-1, ::-1]
    wg = jnp.pad(
        jnp.transpose(flipped, (0, 3, 4, 1, 2, 5)), ((0, 0),) * 4 + ((0, 1), (0, 0))
    ).reshape(2, 576, 128)
    x, cot = (jnp.transpose(one, (2, 1, 0, 3)) for one in (inputs, cotangent))
    bf, sems = jnp.bfloat16, 19 + spaces
    vmem = pl.BlockSpec(memory_space=pltpu.VMEM)
    out, gi, gw = pl.pallas_call(
        functools.partial(kernel, spaces),
        out_shape=(
            jax.ShapeDtypeStruct((rows, planes, count, cols), bf),
            jax.ShapeDtypeStruct((rows, planes, count, cols), bf),
            jax.ShapeDtypeStruct((3, 3, 16, 128), jnp.float32),
        ),
        in_specs=[vmem] * 4,
        out_specs=(vmem,) * 3,
        scratch_shapes=[
            pltpu.VMEM((rows, 4, 4, 32, cols), bf),
            pltpu.VMEM((rows, 4, 4, 32, cols), bf),
            pltpu.VMEM((2, 288, 512), bf),
            pltpu.VMEM((4, 576, 128), bf),
            pltpu.VMEM((rows, 2, 32, cols), bf),
            pltpu.VMEM((rows, 2, 4, 32, cols), bf),
            pltpu.VMEM((rows, 64, cols), jnp.float32),
            pltpu.VMEM((2, 3, 4, 3, 32, 128), bf),
            pltpu.VMEM((3, 4, 3, 32, 128), bf),
            pltpu.VMEM((3, 4, 3, 32, 128), bf),
            pltpu.VMEM((spaces, 3, 3, 16, 128), bf),
            pltpu.VMEM((rows, 2, 32, cols), bf),
            pltpu.SemaphoreType.DMA((sems,)),
            pltpu.SemaphoreType.DMA((sems,)),
            pltpu.SemaphoreType.DMA((4,)),
        ],
        compiler_params=pltpu.CompilerParams(
            collective_id=0, has_side_effects=True, vmem_limit_bytes=48 * 1024 * 1024
        ),
    )(x, cot, wf, wg)
    gw = jnp.transpose(gw.reshape(3, 3, 16, 4, 32)[:, :, :, :3], (2, 1, 0, 3, 4))
    return (
        jnp.transpose(out, (2, 1, 0, 3)),
        jnp.transpose(gi, (2, 1, 0, 3)),
        gw.reshape(16, 27, 32),
    )


def solution(mesh):
    in_specs = (
        P("chan", "space", None, None),
        P(None, None, "chan"),
        P("chan", "space", None, None),
    )
    out_specs = (
        P("chan", "space", None, None),
        P("chan", "space", None, None),
        P("space", None, "chan"),
    )

    def body(inputs, weight, cotangent):
        fits = inputs.shape[0] == 32 and inputs.shape[1] == 2 and inputs.shape[3] == 128
        fits = fits and weight.shape == (128, 27, 32) and mesh.shape["space"] == 8
        return (fused if fits else per_device)(inputs, weight, cotangent)

    return jax.shard_map(
        body, mesh=mesh, in_specs=in_specs, out_specs=out_specs, check_vma=False
    )
```

```python
import functools

import jax
import jax.numpy as jnp
from jax import lax
from jax.experimental import pallas as pl
from jax.experimental.pallas import tpu as pltpu
from jax.sharding import PartitionSpec as P


def padded(cells, sides, width):
    for axis, dim in sides:
        count = lax.axis_size(axis)
        head = lax.slice_in_dim(cells, 0, width, axis=dim)
        tail = lax.slice_in_dim(cells, cells.shape[dim] - width, cells.shape[dim], axis=dim)
        cells = jnp.concatenate(
            [
                lax.ppermute(tail, axis, [(i, (i + 1) % count) for i in range(count)]),
                cells,
                lax.ppermute(head, axis, [((i + 1) % count, i) for i in range(count)]),
            ],
            axis=dim,
        )
    return cells


def tap_offsets():
    return [
        (shift_d, shift_h, shift_w)
        for shift_d in (-1, 0, 1)
        for shift_h in (-1, 0, 1)
        for shift_w in (-1, 0, 1)
    ]


def per_device(inputs, weight, cotangent):
    depth_local = inputs.shape[1]
    moved_inputs, moved_cot = (
        lax.all_to_all(inputs, "chan", split_axis=2, concat_axis=0, tiled=True),
        lax.all_to_all(cotangent, "chan", split_axis=2, concat_axis=0, tiled=True),
    )
    rows_local = moved_inputs.shape[2]
    extended = padded(moved_inputs, (("space", 1), ("chan", 2)), 1)
    filters = lax.all_gather(weight, "chan", axis=2, tiled=True)
    pre_act = jnp.zeros(moved_inputs.shape, jnp.float32)
    for index_tap, (shift_d, shift_h, shift_w) in enumerate(tap_offsets()):
        piece = extended[
            :, 1 + shift_d : 1 + shift_d + depth_local, 1 + shift_h : 1 + shift_h + rows_local
        ]
        piece = jnp.roll(piece, -shift_w, axis=3)
        pre_act = pre_act + jnp.einsum(
            "idhw,io->odhw", piece, filters[:, index_tap, :], preferred_element_type=jnp.float32
        )
    out_local = jnp.maximum(pre_act, 0.0).astype(jnp.bfloat16)
    grad_pre = jnp.where(pre_act > 0, moved_cot.astype(jnp.float32), 0.0).astype(jnp.bfloat16)
    output = lax.all_to_all(out_local, "chan", split_axis=0, concat_axis=2, tiled=True)
    grad_ext = padded(grad_pre, (("space", 1), ("chan", 2)), 1)
    grad_sum = jnp.zeros(moved_inputs.shape, jnp.float32)
    for index_tap, (shift_d, shift_h, shift_w) in enumerate(tap_offsets()):
        piece = grad_ext[
            :, 1 - shift_d : 1 - shift_d + depth_local, 1 - shift_h : 1 - shift_h + rows_local
        ]
        piece = jnp.roll(piece, shift_w, axis=3)
        grad_sum = grad_sum + jnp.einsum(
            "odhw,io->idhw", piece, filters[:, index_tap, :], preferred_element_type=jnp.float32
        )
    grad_inputs = lax.all_to_all(
        grad_sum.astype(jnp.bfloat16), "chan", split_axis=0, concat_axis=2, tiled=True
    )
    tap_list = []
    for index_tap, (shift_d, shift_h, shift_w) in enumerate(tap_offsets()):
        piece = extended[
            :, 1 + shift_d : 1 + shift_d + depth_local, 1 + shift_h : 1 + shift_h + rows_local
        ]
        piece = jnp.roll(piece, -shift_w, axis=3)
        tap_list.append(
            jnp.einsum("idhw,odhw->io", piece, grad_pre, preferred_element_type=jnp.float32)
        )
    partial_sum = lax.psum_scatter(
        jnp.stack(tap_list, axis=1), "space", scatter_dimension=0, tiled=True
    )
    grad_weight = lax.psum_scatter(partial_sum, "chan", scatter_dimension=2, tiled=True)
    return (output, grad_inputs, grad_weight)


MESH = pl.DeviceIdType.MESH
CHUNKS = 4


def stencil(filters, cells, total, first, last, sign):
    rows = total.shape[0]

    @pl.loop(first // 2, last // 2)
    def _(pair):
        right = jnp.concatenate(
            [cells[2 * pair + one].reshape(-1, 128) for one in range(2)], axis=1
        )
        terms = jnp.dot(filters(), right, preferred_element_type=jnp.float32)
        for half in range(2):
            part = terms[:, 128 * half : 128 * half + 128].reshape(3, 3, 64, 128)
            for b in range(3):
                row = lax.rem(2 * pair + half + rows - sign * (b - 1), rows)
                total[row] += (
                    part[b, 1]
                    + pltpu.roll(part[b, 1 - sign], 1, 1)
                    + pltpu.roll(part[b, 1 + sign], 127, 1)
                )


def kernel(
    spaces, x_ref, cot_ref, w_ref, out_ref, gi_ref, gw_ref,
    xg, gp, wf, wg, cot, rolled, total, back, parts, other, sums, landed, part_out,
    send, recv, local,
):
    s, c = lax.axis_index("space"), lax.axis_index("chan")
    x, k = c // 2, lax.rem(c, 2)
    chan = [c, 2 * x + 1 - k, lax.rem(c + 2, 4), 2 * (1 - x) + 1 - k]
    up, down = lax.rem(s + 1, spaces), lax.rem(s + spaces - 1, spaces)
    rows = x_ref.shape[0]
    chunks = CHUNKS
    tall = rows // chunks
    edges = [0] + [tall * q - 2 for q in range(1, chunks)] + [rows]
    base_gp, base = 7 * chunks, 12 * chunks

    barrier = pltpu.get_barrier_semaphore()
    greeted = [(s, other_c) for other_c in chan[1:]]
    greeted += [(side, other_c) for side in (up, down) for other_c in range(4)]
    greeted += [(lax.rem(s + step, spaces), c) for step in range(2, spaces - 1)]
    for device in greeted:
        pl.semaphore_signal(barrier, inc=1, device_id=device, device_id_type=MESH)
    pl.semaphore_wait(barrier, len(greeted))

    sent = []

    def start(src, dst, out_sem, in_sem, device):
        copy = pltpu.make_async_remote_copy(
            src_ref=src, dst_ref=dst, send_sem=send.at[out_sem], recv_sem=recv.at[in_sem],
            device_id=device, device_id_type=MESH,
        )
        copy.start()
        sent.append(copy)

    def wait_in(dst, in_sem):
        pltpu.make_async_copy(dst, dst, recv.at[in_sem]).wait()

    def span(q):
        return pl.ds(tall * q, tall)

    keep = [
        pltpu.make_async_copy(x_ref, xg.at[:, pl.ds(1 - k, 2), c], local.at[0]),
        pltpu.make_async_copy(cot_ref.at[:, k], cot.at[:, k], local.at[1]),
        pltpu.make_async_copy(w_ref.at[:, pl.ds(pl.multiple_of(64 * x, 64), 64)], wg.at[c], local.at[2]),
    ]
    for copy in keep:
        copy.start()
    for q in range(chunks):
        at, mine = 7 * q, x_ref.at[span(q)]
        start(mine, xg.at[span(q), pl.ds(1 - k, 2), c], at + 1, at + 1, (s, chan[2]))
        for plane, side in ((0, down), (1, up)):
            for to_x in range(2):
                start(
                    x_ref.at[span(q), plane], xg.at[span(q), 2 * (1 - plane), c],
                    at + 3 + 2 * plane + to_x, at + 3 + c, (side, 2 * to_x + 1 - plane),
                )
        start(mine, xg.at[span(q), pl.ds(k, 2), c], at, at, (s, chan[1]))
    start(cot_ref.at[:, 1 - k], cot.at[:, k], base, base, (s, chan[1]))

    for tap in range(9):
        turned = jnp.transpose(w_ref[tap].astype(jnp.float32)).astype(jnp.bfloat16)
        for a in range(3):
            wf[tap, k, :, 128 * a : 128 * a + 128] = turned[32 * a : 32 * a + 32]
    start(wf.at[:, k], wf.at[:, k], base + 1, base + 1, (s, chan[1]))
    for j in (2, 3, 1):
        half = pl.ds(pl.multiple_of(64 * (chan[j] // 2), 64), 64)
        start(w_ref.at[:, half], wg.at[c], base + 1 + j, base + 1 + j, (s, chan[j]))

    zero = jnp.zeros((4, 32, 128), jnp.bfloat16)

    @pl.loop(0, rows)
    def _(h):
        gp[h, :, 3] = zero
        rolled[h, :, 3] = zero[:2]
        total[h] = jnp.zeros((64, 128), jnp.float32)
        back[h] = jnp.zeros((64, 128), jnp.float32)

    def segment(q):
        return pl.ds(edges[q], edges[q + 1] - edges[q])

    def place(q, slot, of_x=x):
        return gp.at[segment(q), pl.ds(2 * of_x, 2), slot]

    side = lax.rem(s + spaces + 2 * k - 1, spaces)

    for copy in keep:
        copy.wait()
    for q in range(chunks):
        at = 7 * q
        came = xg.at[span(q), pl.ds(1 - k, 2), chan[2]]
        wait_in(came, at + 1)
        start(came, xg.at[span(q), pl.ds(k, 2), chan[2]], at + 2, at + 2, (s, chan[1]))
        wait_in(xg.at[span(q), pl.ds(1 - k, 2), chan[1]], at)
        for from_c in range(4):
            wait_in(xg.at[span(q), 2 * k, from_c], at + 3 + from_c)
        wait_in(xg.at[span(q), pl.ds(1 - k, 2), chan[3]], at + 2)
        if q == 0:
            wait_in(wf.at[:, 1 - k], base + 1)
        stencil(lambda: wf[...].reshape(576, 384), xg, total, tall * q, tall * q + tall, 1)
        if q == 0:
            wait_in(cot.at[:, 1 - k], base)

        @pl.loop(edges[q], edges[q + 1])
        def _(r):
            h = lax.rem(r + 1, rows)
            pre = total[h].reshape(2, 32, 128)
            part_out[h] = jnp.maximum(pre, 0.0).astype(jnp.bfloat16)
            grad = jnp.where(pre > 0, cot[h].astype(jnp.float32), 0.0)
            gp[r, pl.ds(2 * x, 2), 1] = grad.astype(jnp.bfloat16)
            flat = grad.reshape(64, 128)
            rolled[h, :, 0] = pltpu.roll(flat, 127, 1).reshape(2, 32, 128).astype(jnp.bfloat16)
            rolled[h, :, 1] = grad.astype(jnp.bfloat16)
            rolled[h, :, 2] = pltpu.roll(flat, 1, 1).reshape(2, 32, 128).astype(jnp.bfloat16)

        at = base_gp + 5 * q
        start(place(q, 1), place(q, 1), at + 1, at + 1, (s, chan[2]))
        for to_x in range(2):
            start(place(q, 1), place(q, 2 * k), at + 3 + to_x, at + 3 + x, (side, 2 * to_x + 1 - k))
        start(place(q, 1), place(q, 2 * (1 - k)), at, at, (s, chan[1]))

    start(part_out.at[:, 1 - k], out_ref.at[:, k], base + 5, base + 5, (s, chan[1]))
    copy_out = pltpu.make_async_copy(part_out.at[:, k], out_ref.at[:, k], local.at[0])
    copy_out.start()

    def relay(q):
        at = base_gp + 5 * q
        came = place(q, 1, 1 - x)
        wait_in(came, at + 1)
        start(came, place(q, 2 * (1 - k), 1 - x), at + 2, at + 2, (s, chan[1]))

    def filter_sums(b):
        left = jnp.concatenate(
            [xg[(h + b - 1) % rows].reshape(384, 128) for h in range(rows)], axis=1
        )
        right = jnp.concatenate([rolled[h].reshape(256, 128) for h in range(rows)], axis=1)
        got = lax.dot_general(
            left, right, (((1,), (1,)), ((), ())), preferred_element_type=jnp.float32
        ).astype(jnp.bfloat16)
        for half in range(2):
            parts[half, b] = got[:, 128 * half : 128 * half + 128].reshape(3, 128, 128)

    for q in range(chunks - 2):
        relay(q)
    filter_sums(0)
    relay(chunks - 2)
    filter_sums(1)
    filter_sums(2)
    start(parts.at[1 - k], other, base + 6, base + 6, (s, chan[1]))
    relay(chunks - 1)
    wait_in(other, base + 6)

    @pl.loop(0, 3)
    def _(b):
        sums[b] = (
            parts[k, b].astype(jnp.float32) + other[b].astype(jnp.float32)
        ).astype(jnp.bfloat16)

    def block(owner):
        return sums.at[:, :, pl.ds(pl.multiple_of(16 * owner, 16), 16)]

    for step in range(1, spaces):
        owner = lax.rem(s + step, spaces)
        start(block(owner), landed.at[step], base + 6 + step, base + 6 + step, (owner, c))
    own = pltpu.make_async_copy(block(s), landed.at[0], local.at[1])
    own.start()

    for j in (1, 2, 3):
        wait_in(wg.at[chan[j]], base + 1 + j)
    for q in range(chunks):
        at = base_gp + 5 * q
        wait_in(place(q, 2 * k), at)
        wait_in(place(q, 2 * k, 1 - x), at + 2)
        for from_x in range(2):
            wait_in(place(q, 2 * (1 - k), from_x), at + 3 + from_x)
        stencil(
            lambda: jnp.concatenate([wg[j].reshape(576, 128) for j in range(4)], axis=1),
            gp, back, edges[q], edges[q + 1], -1,
        )

    @pl.loop(0, rows)
    def _(r):
        rolled[lax.rem(r + 1, rows), :, 0] = back[r].reshape(2, 32, 128).astype(jnp.bfloat16)

    last = base + 6 + spaces
    start(rolled.at[:, 1 - k, 0], gi_ref.at[:, k], last, last, (s, chan[1]))
    copy_gi = pltpu.make_async_copy(rolled.at[:, k, 0], gi_ref.at[:, k], local.at[2])
    copy_gi.start()

    own.wait()
    for step in range(1, spaces):
        wait_in(landed.at[step], base + 6 + step)
    whole = landed[0].astype(jnp.float32)
    for step in range(1, spaces):
        whole = whole + landed[step].astype(jnp.float32)
    gw_ref[...] = whole

    copy_out.wait()
    copy_gi.wait()
    wait_in(out_ref.at[:, 1 - k], base + 5)
    wait_in(gi_ref.at[:, 1 - k], last)
    for copy in sent:
        copy.wait_send()


def fused(inputs, weight, cotangent):
    spaces = lax.axis_size("space")
    count, planes, rows, cols = inputs.shape
    bf, sems = jnp.bfloat16, 12 * CHUNKS + 7 + spaces
    taps = jnp.transpose(weight, (1, 0, 2)).reshape(3, 9, 128, 32)
    filters = jnp.concatenate([taps[0], taps[1], taps[2], jnp.zeros_like(taps[0])], axis=2)
    x, cot = (jnp.transpose(one, (2, 1, 0, 3)) for one in (inputs, cotangent))
    vmem = pl.BlockSpec(memory_space=pltpu.VMEM)
    out, gi, gw = pl.pallas_call(
        functools.partial(kernel, spaces),
        out_shape=(
            jax.ShapeDtypeStruct((rows, planes, count, cols), bf),
            jax.ShapeDtypeStruct((rows, planes, count, cols), bf),
            jax.ShapeDtypeStruct((3, 3, 16, 128), jnp.float32),
        ),
        in_specs=[vmem] * 3,
        out_specs=(vmem,) * 3,
        scratch_shapes=[
            pltpu.VMEM((rows, 3, 4, 32, cols), bf),
            pltpu.VMEM((rows, 4, 4, 32, cols), bf),
            pltpu.VMEM((9, 2, 32, 384), bf),
            pltpu.VMEM((4, 9, 64, 128), bf),
            pltpu.VMEM((rows, 2, 32, cols), bf),
            pltpu.VMEM((rows, 2, 4, 32, cols), bf),
            pltpu.VMEM((rows, 64, cols), jnp.float32),
            pltpu.VMEM((rows, 64, cols), jnp.float32),
            pltpu.VMEM((2, 3, 3, 128, 128), bf),
            pltpu.VMEM((3, 3, 128, 128), bf),
            pltpu.VMEM((3, 3, 128, 128), bf),
            pltpu.VMEM((spaces, 3, 3, 16, 128), bf),
            pltpu.VMEM((rows, 2, 32, cols), bf),
            pltpu.SemaphoreType.DMA((sems,)),
            pltpu.SemaphoreType.DMA((sems,)),
            pltpu.SemaphoreType.DMA((3,)),
        ],
        compiler_params=pltpu.CompilerParams(
            collective_id=0, has_side_effects=True, vmem_limit_bytes=48 * 1024 * 1024
        ),
    )(x, cot, filters)
    gw = jnp.transpose(gw.reshape(3, 3, 16, 4, 32)[:, :, :, :3], (2, 1, 0, 3, 4))
    return (
        jnp.transpose(out, (2, 1, 0, 3)),
        jnp.transpose(gi, (2, 1, 0, 3)),
        gw.reshape(16, 27, 32),
    )


def solution(mesh):
    in_specs = (
        P("chan", "space", None, None),
        P(None, None, "chan"),
        P("chan", "space", None, None),
    )
    out_specs = (
        P("chan", "space", None, None),
        P("chan", "space", None, None),
        P("space", None, "chan"),
    )

    def body(inputs, weight, cotangent):
        fits = inputs.shape[0] == 32 and inputs.shape[1] == 2 and inputs.shape[3] == 128
        fits = fits and weight.shape == (128, 27, 32) and mesh.shape["space"] == 8
        return (fused if fits else per_device)(inputs, weight, cotangent)

    return jax.shard_map(
        body, mesh=mesh, in_specs=in_specs, out_specs=out_specs, check_vma=False
    )
```

```python
import functools

import jax
import jax.numpy as jnp
from jax import lax
from jax.experimental import pallas as pl
from jax.experimental.pallas import tpu as pltpu
from jax.sharding import PartitionSpec as P


def padded(cells, sides, width):
    for axis, dim in sides:
        count = lax.axis_size(axis)
        head = lax.slice_in_dim(cells, 0, width, axis=dim)
        tail = lax.slice_in_dim(cells, cells.shape[dim] - width, cells.shape[dim], axis=dim)
        cells = jnp.concatenate(
            [
                lax.ppermute(tail, axis, [(i, (i + 1) % count) for i in range(count)]),
                cells,
                lax.ppermute(head, axis, [((i + 1) % count, i) for i in range(count)]),
            ],
            axis=dim,
        )
    return cells


def tap_offsets():
    return [
        (shift_d, shift_h, shift_w)
        for shift_d in (-1, 0, 1)
        for shift_h in (-1, 0, 1)
        for shift_w in (-1, 0, 1)
    ]


def per_device(inputs, weight, cotangent):
    depth_local = inputs.shape[1]
    moved_inputs, moved_cot = (
        lax.all_to_all(inputs, "chan", split_axis=2, concat_axis=0, tiled=True),
        lax.all_to_all(cotangent, "chan", split_axis=2, concat_axis=0, tiled=True),
    )
    rows_local = moved_inputs.shape[2]
    extended = padded(moved_inputs, (("space", 1), ("chan", 2)), 1)
    filters = lax.all_gather(weight, "chan", axis=2, tiled=True)
    pre_act = jnp.zeros(moved_inputs.shape, jnp.float32)
    for index_tap, (shift_d, shift_h, shift_w) in enumerate(tap_offsets()):
        piece = extended[
            :, 1 + shift_d : 1 + shift_d + depth_local, 1 + shift_h : 1 + shift_h + rows_local
        ]
        piece = jnp.roll(piece, -shift_w, axis=3)
        pre_act = pre_act + jnp.einsum(
            "idhw,io->odhw", piece, filters[:, index_tap, :], preferred_element_type=jnp.float32
        )
    out_local = jnp.maximum(pre_act, 0.0).astype(jnp.bfloat16)
    grad_pre = jnp.where(pre_act > 0, moved_cot.astype(jnp.float32), 0.0).astype(jnp.bfloat16)
    output = lax.all_to_all(out_local, "chan", split_axis=0, concat_axis=2, tiled=True)
    grad_ext = padded(grad_pre, (("space", 1), ("chan", 2)), 1)
    grad_sum = jnp.zeros(moved_inputs.shape, jnp.float32)
    for index_tap, (shift_d, shift_h, shift_w) in enumerate(tap_offsets()):
        piece = grad_ext[
            :, 1 - shift_d : 1 - shift_d + depth_local, 1 - shift_h : 1 - shift_h + rows_local
        ]
        piece = jnp.roll(piece, shift_w, axis=3)
        grad_sum = grad_sum + jnp.einsum(
            "odhw,io->idhw", piece, filters[:, index_tap, :], preferred_element_type=jnp.float32
        )
    grad_inputs = lax.all_to_all(
        grad_sum.astype(jnp.bfloat16), "chan", split_axis=0, concat_axis=2, tiled=True
    )
    tap_list = []
    for index_tap, (shift_d, shift_h, shift_w) in enumerate(tap_offsets()):
        piece = extended[
            :, 1 + shift_d : 1 + shift_d + depth_local, 1 + shift_h : 1 + shift_h + rows_local
        ]
        piece = jnp.roll(piece, -shift_w, axis=3)
        tap_list.append(
            jnp.einsum("idhw,odhw->io", piece, grad_pre, preferred_element_type=jnp.float32)
        )
    partial_sum = lax.psum_scatter(
        jnp.stack(tap_list, axis=1), "space", scatter_dimension=0, tiled=True
    )
    grad_weight = lax.psum_scatter(partial_sum, "chan", scatter_dimension=2, tiled=True)
    return (output, grad_inputs, grad_weight)


MESH = pl.DeviceIdType.MESH
CHUNKS = 2


def stencil(filters, cells, total, first, last, sign):
    rows = total.shape[0]

    @pl.loop(first // 2, last // 2)
    def _(pair):
        right = jnp.concatenate(
            [cells[2 * pair + one].reshape(-1, 128) for one in range(2)], axis=1
        )
        terms = jnp.dot(filters(), right, preferred_element_type=jnp.float32)
        for half in range(2):
            part = terms[:, 128 * half : 128 * half + 128].reshape(3, 3, 64, 128)
            for b in range(3):
                row = lax.rem(2 * pair + half + rows - sign * (b - 1), rows)
                total[row] += (
                    part[b, 1]
                    + pltpu.roll(part[b, 1 - sign], 1, 1)
                    + pltpu.roll(part[b, 1 + sign], 127, 1)
                )


def kernel(
    spaces, x_ref, cot_ref, w_ref, out_ref, gi_ref, gw_ref,
    xg, gp, wf, wg, cot, rolled, total, back, parts, other, sums, landed, part_out,
    send, recv, local,
):
    s, c = lax.axis_index("space"), lax.axis_index("chan")
    x, k = c // 2, lax.rem(c, 2)
    chan = [c, 2 * x + 1 - k, lax.rem(c + 2, 4), 2 * (1 - x) + 1 - k]
    up, down = lax.rem(s + 1, spaces), lax.rem(s + spaces - 1, spaces)
    rows = x_ref.shape[0]
    chunks = CHUNKS
    tall = rows // chunks
    edges = [0] + [tall * q - 2 for q in range(1, chunks)] + [rows]
    base_gp, base = 7 * chunks, 12 * chunks

    barrier = pltpu.get_barrier_semaphore()
    greeted = [(s, other_c) for other_c in chan[1:]]
    greeted += [(side, other_c) for side in (up, down) for other_c in range(4)]
    greeted += [(lax.rem(s + step, spaces), c) for step in range(2, spaces - 1)]
    for device in greeted:
        pl.semaphore_signal(barrier, inc=1, device_id=device, device_id_type=MESH)
    pl.semaphore_wait(barrier, len(greeted))

    sent = []

    def start(src, dst, out_sem, in_sem, device):
        copy = pltpu.make_async_remote_copy(
            src_ref=src, dst_ref=dst, send_sem=send.at[out_sem], recv_sem=recv.at[in_sem],
            device_id=device, device_id_type=MESH,
        )
        copy.start()
        sent.append(copy)

    def wait_in(dst, in_sem):
        pltpu.make_async_copy(dst, dst, recv.at[in_sem]).wait()

    def span(q):
        return pl.ds(tall * q, tall)

    keep = [
        pltpu.make_async_copy(x_ref, xg.at[:, pl.ds(1 - k, 2), c], local.at[0]),
        pltpu.make_async_copy(cot_ref.at[:, k], cot.at[:, k], local.at[1]),
        pltpu.make_async_copy(w_ref.at[:, pl.ds(pl.multiple_of(64 * x, 64), 64)], wg.at[c], local.at[2]),
    ]
    for copy in keep:
        copy.start()
    for q in range(chunks):
        at, mine = 7 * q, x_ref.at[span(q)]
        start(mine, xg.at[span(q), pl.ds(1 - k, 2), c], at + 1, at + 1, (s, chan[2]))
        for plane, side in ((0, down), (1, up)):
            for to_x in range(2):
                start(
                    x_ref.at[span(q), plane], xg.at[span(q), 2 * (1 - plane), c],
                    at + 3 + 2 * plane + to_x, at + 3 + c, (side, 2 * to_x + 1 - plane),
                )
        start(mine, xg.at[span(q), pl.ds(k, 2), c], at, at, (s, chan[1]))
    start(cot_ref.at[:, 1 - k], cot.at[:, k], base, base, (s, chan[1]))

    for tap in range(9):
        turned = jnp.transpose(w_ref[tap].astype(jnp.float32)).astype(jnp.bfloat16)
        for a in range(3):
            wf[tap, k, :, 128 * a : 128 * a + 128] = turned[32 * a : 32 * a + 32]
    start(wf.at[:, k], wf.at[:, k], base + 1, base + 1, (s, chan[1]))
    for j in (1, 2):
        half = pl.ds(pl.multiple_of(64 * (chan[j] // 2), 64), 64)
        start(w_ref.at[:, half], wg.at[c], base + 1 + j, base + 1 + j, (s, chan[j]))

    zero = jnp.zeros((4, 32, 128), jnp.bfloat16)

    @pl.loop(0, rows)
    def _(h):
        gp[h, :, 3] = zero
        rolled[h, :, 3] = zero[:2]
        total[h] = jnp.zeros((64, 128), jnp.float32)
        back[h] = jnp.zeros((64, 128), jnp.float32)

    def segment(q):
        return pl.ds(edges[q], edges[q + 1] - edges[q])

    def place(q, slot, of_x=x):
        return gp.at[segment(q), pl.ds(2 * of_x, 2), slot]

    side = lax.rem(s + spaces + 2 * k - 1, spaces)

    for copy in keep:
        copy.wait()
    for q in range(chunks):
        at = 7 * q
        came = xg.at[span(q), pl.ds(1 - k, 2), chan[2]]
        wait_in(came, at + 1)
        start(came, xg.at[span(q), pl.ds(k, 2), chan[2]], at + 2, at + 2, (s, chan[1]))
        wait_in(xg.at[span(q), pl.ds(1 - k, 2), chan[1]], at)
        for from_c in range(4):
            wait_in(xg.at[span(q), 2 * k, from_c], at + 3 + from_c)
        wait_in(xg.at[span(q), pl.ds(1 - k, 2), chan[3]], at + 2)
        if q == 0:
            wait_in(wf.at[:, 1 - k], base + 1)
        stencil(lambda: wf[...].reshape(576, 384), xg, total, tall * q, tall * q + tall, 1)
        if q == 0:
            wait_in(cot.at[:, 1 - k], base)

        @pl.loop(edges[q], edges[q + 1])
        def _(r):
            h = lax.rem(r + 1, rows)
            pre = total[h].reshape(2, 32, 128)
            part_out[h] = jnp.maximum(pre, 0.0).astype(jnp.bfloat16)
            grad = jnp.where(pre > 0, cot[h].astype(jnp.float32), 0.0)
            gp[r, pl.ds(2 * x, 2), 1] = grad.astype(jnp.bfloat16)
            flat = grad.reshape(64, 128)
            rolled[h, :, 0] = pltpu.roll(flat, 127, 1).reshape(2, 32, 128).astype(jnp.bfloat16)
            rolled[h, :, 1] = grad.astype(jnp.bfloat16)
            rolled[h, :, 2] = pltpu.roll(flat, 1, 1).reshape(2, 32, 128).astype(jnp.bfloat16)

        at = base_gp + 5 * q
        start(place(q, 1), place(q, 1), at + 1, at + 1, (s, chan[2]))
        for to_x in range(2):
            start(place(q, 1), place(q, 2 * k), at + 3 + to_x, at + 3 + x, (side, 2 * to_x + 1 - k))
        start(place(q, 1), place(q, 2 * (1 - k)), at, at, (s, chan[1]))

    start(part_out.at[:, 1 - k], out_ref.at[:, k], base + 5, base + 5, (s, chan[1]))
    copy_out = pltpu.make_async_copy(part_out.at[:, k], out_ref.at[:, k], local.at[0])
    copy_out.start()

    def relay(q):
        at = base_gp + 5 * q
        came = place(q, 1, 1 - x)
        wait_in(came, at + 1)
        start(came, place(q, 2 * (1 - k), 1 - x), at + 2, at + 2, (s, chan[1]))

    def filter_sums(b):
        left = jnp.concatenate(
            [xg[(h + b - 1) % rows].reshape(384, 128) for h in range(rows)], axis=1
        )
        right = jnp.concatenate([rolled[h].reshape(256, 128) for h in range(rows)], axis=1)
        got = lax.dot_general(
            left, right, (((1,), (1,)), ((), ())), preferred_element_type=jnp.float32
        ).astype(jnp.bfloat16)
        for half in range(2):
            parts[half, b] = got[:, 128 * half : 128 * half + 128].reshape(3, 128, 128)

    wait_in(wg.at[chan[2]], base + 3)
    start(wg.at[chan[2]], wg.at[chan[2]], base + 4, base + 4, (s, chan[1]))
    for q in range(chunks - 2):
        relay(q)
    filter_sums(0)
    relay(chunks - 2)
    filter_sums(1)
    filter_sums(2)
    start(parts.at[1 - k], other, base + 6, base + 6, (s, chan[1]))
    relay(chunks - 1)
    wait_in(other, base + 6)

    @pl.loop(0, 3)
    def _(b):
        sums[b] = (
            parts[k, b].astype(jnp.float32) + other[b].astype(jnp.float32)
        ).astype(jnp.bfloat16)

    def block(owner):
        return sums.at[:, :, pl.ds(pl.multiple_of(16 * owner, 16), 16)]

    for step in range(1, spaces):
        owner = lax.rem(s + step, spaces)
        start(block(owner), landed.at[step], base + 6 + step, base + 6 + step, (owner, c))
    own = pltpu.make_async_copy(block(s), landed.at[0], local.at[1])
    own.start()

    for j in (1, 3):
        wait_in(wg.at[chan[j]], base + 1 + j)
    for q in range(chunks):
        at = base_gp + 5 * q
        wait_in(place(q, 2 * k), at)
        wait_in(place(q, 2 * k, 1 - x), at + 2)
        for from_x in range(2):
            wait_in(place(q, 2 * (1 - k), from_x), at + 3 + from_x)
        stencil(
            lambda: jnp.concatenate([wg[j].reshape(576, 128) for j in range(4)], axis=1),
            gp, back, edges[q], edges[q + 1], -1,
        )

    @pl.loop(0, rows)
    def _(r):
        rolled[lax.rem(r + 1, rows), :, 0] = back[r].reshape(2, 32, 128).astype(jnp.bfloat16)

    last = base + 6 + spaces
    start(rolled.at[:, 1 - k, 0], gi_ref.at[:, k], last, last, (s, chan[1]))
    copy_gi = pltpu.make_async_copy(rolled.at[:, k, 0], gi_ref.at[:, k], local.at[2])
    copy_gi.start()

    own.wait()
    for step in range(1, spaces):
        wait_in(landed.at[step], base + 6 + step)
    whole = landed[0].astype(jnp.float32)
    for step in range(1, spaces):
        whole = whole + landed[step].astype(jnp.float32)
    gw_ref[...] = whole

    copy_out.wait()
    copy_gi.wait()
    wait_in(out_ref.at[:, 1 - k], base + 5)
    wait_in(gi_ref.at[:, 1 - k], last)
    for copy in sent:
        copy.wait_send()


def fused(inputs, weight, cotangent):
    spaces = lax.axis_size("space")
    count, planes, rows, cols = inputs.shape
    bf, sems = jnp.bfloat16, 12 * CHUNKS + 7 + spaces
    taps = jnp.transpose(weight, (1, 0, 2)).reshape(3, 9, 128, 32)
    filters = jnp.concatenate([taps[0], taps[1], taps[2], jnp.zeros_like(taps[0])], axis=2)
    x, cot = (jnp.transpose(one, (2, 1, 0, 3)) for one in (inputs, cotangent))
    vmem = pl.BlockSpec(memory_space=pltpu.VMEM)
    out, gi, gw = pl.pallas_call(
        functools.partial(kernel, spaces),
        out_shape=(
            jax.ShapeDtypeStruct((rows, planes, count, cols), bf),
            jax.ShapeDtypeStruct((rows, planes, count, cols), bf),
            jax.ShapeDtypeStruct((3, 3, 16, 128), jnp.float32),
        ),
        in_specs=[vmem] * 3,
        out_specs=(vmem,) * 3,
        scratch_shapes=[
            pltpu.VMEM((rows, 3, 4, 32, cols), bf),
            pltpu.VMEM((rows, 4, 4, 32, cols), bf),
            pltpu.VMEM((9, 2, 32, 384), bf),
            pltpu.VMEM((4, 9, 64, 128), bf),
            pltpu.VMEM((rows, 2, 32, cols), bf),
            pltpu.VMEM((rows, 2, 4, 32, cols), bf),
            pltpu.VMEM((rows, 64, cols), jnp.float32),
            pltpu.VMEM((rows, 64, cols), jnp.float32),
            pltpu.VMEM((2, 3, 3, 128, 128), bf),
            pltpu.VMEM((3, 3, 128, 128), bf),
            pltpu.VMEM((3, 3, 128, 128), bf),
            pltpu.VMEM((spaces, 3, 3, 16, 128), bf),
            pltpu.VMEM((rows, 2, 32, cols), bf),
            pltpu.SemaphoreType.DMA((sems,)),
            pltpu.SemaphoreType.DMA((sems,)),
            pltpu.SemaphoreType.DMA((3,)),
        ],
        compiler_params=pltpu.CompilerParams(
            collective_id=0, has_side_effects=True, vmem_limit_bytes=48 * 1024 * 1024
        ),
    )(x, cot, filters)
    gw = jnp.transpose(gw.reshape(3, 3, 16, 4, 32)[:, :, :, :3], (2, 1, 0, 3, 4))
    return (
        jnp.transpose(out, (2, 1, 0, 3)),
        jnp.transpose(gi, (2, 1, 0, 3)),
        gw.reshape(16, 27, 32),
    )


def solution(mesh):
    in_specs = (
        P("chan", "space", None, None),
        P(None, None, "chan"),
        P("chan", "space", None, None),
    )
    out_specs = (
        P("chan", "space", None, None),
        P("chan", "space", None, None),
        P("space", None, "chan"),
    )

    def body(inputs, weight, cotangent):
        fits = inputs.shape[0] == 32 and inputs.shape[1] == 2 and inputs.shape[3] == 128
        fits = fits and weight.shape == (128, 27, 32) and mesh.shape["space"] == 8
        return (fused if fits else per_device)(inputs, weight, cotangent)

    return jax.shard_map(
        body, mesh=mesh, in_specs=in_specs, out_specs=out_specs, check_vma=False
    )
```
